32 devices in a mesh: tm: 8 (over y, x, core), dp: 4 (over z).
Axes of the slice: x: 2, y: 2, z: 4, core: 2. Of those that a mesh axis runs over, the one named last changes fastest.
Arguments:
- queries: bfloat16 [4, 6144, 1536], P('dp', 'tm'), may hold values from -256 to 256
- key_states: bfloat16 [4, 6144, 1536], P('dp', 'tm'), may hold values from -4 to 4
- value_states: bfloat16 [4, 6144, 1536], P('dp', 'tm'), may hold values from -6 to 6
- out_grad: bfloat16 [4, 6144, 1536], P('dp', 'tm'), may hold values from -12 to 12
- out_weight: bfloat16 [1536, 1536], P('dp'), may hold values from -0.15625 to 0.15625
- win_time: int32 [4, 16, 3], P('dp', 'tm'), may hold values from -1 to 1, as said below
- win_space: int32 [4, 16, 3], P('dp', 'tm'), may hold values from 0 to 1
- tile_len: int32 [4, 16], P('dp'), may hold values from 192 to 384, as said below
Outputs:
- query_grad: bfloat16 [4, 6144, 1536], P('dp', 'tm')
- key_grad: bfloat16 [4, 6144, 1536], P('dp', 'tm')
- value_grad: bfloat16 [4, 6144, 1536], P('dp', 'tm')
- weight_grad: float32 [1536, 1536], P(('tm', 'dp'))
The draws below stay inside these ranges and needn't reach their ends.
Inputs may be any that keep to these rules, and one draw needn't show every extreme that they name: `win_time`: the 3 tiles that a query tile's further slots name are distinct and never the query tile itself; the offset counts slabs along the loop of 8 slabs. `tile_len`: the valid tokens are the first ones of the tile.
All inputs are finite; a program needn't handle non-finite values.
Results may differ from the reference program's by a relative error of at most 0.015.
Values may be sent and summed in bfloat16 or wider, within the bound.
A program may use at most 192 MiB of HBM per device.

```python
import math
import jax
import jax.numpy as jnp
from jax import lax

HEAD = 128
DOUT = 1536
TILE = 384
W = 4
TPD = 2
HD = 1536
CLIPS = 4
TOKENS = 6144
N_TM = 8


def shared_keys(key):
    base = jnp.clip(jax.random.normal(jax.random.fold_in(key, 1), (CLIPS, TOKENS, HD), jnp.float32), -4.0, 4.0)
    return base


def window_codes(key):
    tile_total = TOKENS // TILE
    pool_count = 3 * TPD
    shape = (CLIPS, tile_total, pool_count)
    slot_id = lax.broadcasted_iota(jnp.int32, shape, 2)
    tile_id = lax.broadcasted_iota(jnp.int32, shape, 1)
    clip_id = lax.broadcasted_iota(jnp.int32, shape, 0)
    ranked = jax.random.randint(jax.random.fold_in(key, 7), shape, 0, 65536) * pool_count + slot_id
    ranked = jnp.where(slot_id == TPD + tile_id % TPD, 2 ** 30, ranked)
    first = (clip_id == 0) & (tile_id == 0)
    ranked = jnp.where(first & (slot_id == 0), -3, ranked)
    ranked = jnp.where(first & (slot_id == 2 * TPD), -2, ranked)
    ranked = jnp.where(first & (slot_id == 3 * TPD - 1), -1, ranked)
    ordered = jnp.argsort(ranked, axis=2, stable=True)
    return ordered[:, :, :W - 1].astype(jnp.int32)


def draw_queries(key, part):
    key = jax.random.fold_in(key, 22)
    own = jnp.clip(2.0 * jax.random.normal(key, (CLIPS, TOKENS, HD), jnp.float32), -8.0, 8.0)
    return own.astype(jnp.bfloat16)


def draw_key_states(key, part):
    base = shared_keys(key)
    return base.astype(jnp.bfloat16)


def draw_win_time(key, part):
    ordered = window_codes(key)
    return (ordered // TPD - 1).astype(jnp.int32)


def draw_win_space(key, part):
    ordered = window_codes(key)
    return (ordered % TPD).astype(jnp.int32)


def draw_tile_len(key, part):
    key = jax.random.fold_in(key, 31)
    shape = (CLIPS, TOKENS // TILE)
    lengths = jax.random.randint(key, shape, TILE // 2, TILE + 1)
    position = lax.broadcasted_iota(jnp.int32, shape, 1)
    lengths = jnp.where(position == 0, TILE, lengths)
    lengths = jnp.where(position == 1, TILE // 2, lengths)
    return lengths.astype(jnp.int32)


def spiked(values, rng, source, target, shards_of, factor):
    owner, partner = [(jnp.arange(values.shape[axis_at]) // (values.shape[axis_at] // shards_of)).reshape([-1 if axis == axis_at else 1 for axis in range(values.ndim)]) for axis_at in (source, target)]
    chosen = jax.random.permutation(rng, shards_of)[partner]
    strong = (owner == chosen) | (owner == (partner + shards_of // 2) % shards_of)
    return jnp.where(strong, factor * values, values)


def block_scale(rng, shape, cuts, least, largest):
    def one(dim, shards_of):
        heights = jax.random.uniform(jax.random.fold_in(jax.random.fold_in(rng, 6), dim), (shards_of,), jnp.float32, least / len(cuts), largest / len(cuts))
        return jnp.repeat(jnp.exp(heights), shape[dim] // shards_of).reshape((-1,) + (1,) * (len(shape) - dim - 1))

    gain = one(*cuts[0])
    for cut in cuts[1:]:
        gain = gain * one(*cut)
    return gain


def centred(stream_key, shape, deviation, limit, split=(), kind=jnp.bfloat16):
    factor_of = block_scale(stream_key, shape, split, -0.22, 0.18) if split else 1.0
    entries = jax.random.normal(stream_key, shape, jnp.float32) * deviation * factor_of
    return jnp.minimum(jnp.maximum(entries, -limit), limit).astype(kind)


def bell_draw_with(own_key, dims, width, reach, shards, heavy, held_as=jnp.bfloat16):
    result = width * jax.random.normal(own_key, dims, jnp.float32)
    if shards:
        result = result * block_scale(own_key, dims, shards, -0.22, 0.18)
    return jnp.clip(spiked(result, jax.random.fold_in(own_key, 3), *heavy), -reach, reach).astype(held_as)


def setup_inputs(seed: int = 0) -> dict:
    seeds = jax.random.split(jax.random.key(seed), 9)
    return {
        "queries": draw_queries(jax.random.fold_in(seeds[8], 71), 0),
        "key_states": draw_key_states(jax.random.fold_in(seeds[8], 71), 0),
        "value_states": centred(seeds[2], (CLIPS, TOKENS, HD), 1.0, 6.0, ((0, 4), (1, 8))),
        "out_grad": bell_draw_with(seeds[3], (CLIPS, TOKENS, DOUT), 2.0, 12.0, ((0, 4), (1, 8)), (1, 2, 8, 2.0)),
        "out_weight": centred(seeds[4], (DOUT, HD), DOUT ** -0.5, 0.15625, ((0, 4),)),
        "win_time": draw_win_time(jax.random.fold_in(seeds[8], 71), 0),
        "win_space": draw_win_space(jax.random.fold_in(seeds[8], 71), 0),
        "tile_len": draw_tile_len(jax.random.fold_in(seeds[8], 71), 0),
    }


def slab_grads(query_tiles, dout_tiles, pool_key, pool_value, pool_len, slot_codes):
    tile_count, tile_size, features = query_tiles.shape
    pool_count = pool_key.shape[0]
    slot_count = slot_codes.shape[1]
    head_count = features // HEAD
    scaling = 1.0 / math.sqrt(HEAD)
    select = slot_codes[:, :, None] == lax.broadcasted_iota(jnp.int32, (tile_count, slot_count, pool_count), 2)
    lengths = lax.optimization_barrier(jnp.sum(jnp.where(select, pool_len[None, None, :], 0), axis=2))
    usable = lax.broadcasted_iota(jnp.int32, (tile_count, slot_count, tile_size), 2) < lengths[:, :, None]
    usable = usable.reshape(tile_count, 1, slot_count * tile_size)
    flat_codes = slot_codes.reshape(-1)
    window_key = jnp.take(pool_key, flat_codes, axis=0).reshape(tile_count, slot_count * tile_size, head_count, HEAD)
    window_value = jnp.take(pool_value, flat_codes, axis=0).reshape(tile_count, slot_count * tile_size, head_count, HEAD)
    select_f = select.astype(jnp.float32)

    def per_head(stacked):
        query_head, dout_head, key_head, value_head = stacked
        query_f = query_head.astype(jnp.float32)
        dout_f = dout_head.astype(jnp.float32)
        key_f = key_head.astype(jnp.float32)
        value_f = value_head.astype(jnp.float32)
        scores = jnp.einsum('tqd,tkd->tqk', query_f, key_f) * scaling
        scores = jnp.where(usable, scores, -jnp.inf)
        row_max = lax.optimization_barrier(jnp.max(scores, axis=2, keepdims=True))
        exponent = jnp.exp(scores - row_max)
        probs_f = exponent / lax.optimization_barrier(jnp.sum(exponent, axis=2, keepdims=True))
        weights = probs_f.astype(jnp.bfloat16)
        weights_f = weights.astype(jnp.float32)
        attended = jnp.einsum('tqk,tkd->tqd', weights_f, value_f).astype(jnp.bfloat16)
        attended = lax.optimization_barrier(attended)
        prob_grad = jnp.einsum('tqd,tkd->tqk', dout_f, value_f)
        rowdot = lax.optimization_barrier(jnp.sum(dout_f * attended.astype(jnp.float32), axis=2, keepdims=True))
        dscore = (probs_f * (prob_grad - rowdot)).astype(jnp.bfloat16)
        dscore_f = dscore.astype(jnp.float32)
        query_out = (jnp.einsum('tqk,tkd->tqd', dscore_f, key_f) * scaling).astype(jnp.bfloat16)
        key_part = jnp.einsum('tqk,tqd->tkd', dscore_f, query_f) * scaling
        value_part = jnp.einsum('tqk,tqd->tkd', weights_f, dout_f)
        key_pool = jnp.einsum('tsp,tskd->pkd', select_f, key_part.reshape(tile_count, slot_count, tile_size, HEAD), precision=lax.Precision.HIGHEST)
        value_pool = jnp.einsum('tsp,tskd->pkd', select_f, value_part.reshape(tile_count, slot_count, tile_size, HEAD), precision=lax.Precision.HIGHEST)
        return (query_out, attended, key_pool, value_pool)
    heads_first = (jnp.moveaxis(query_tiles.reshape(tile_count, tile_size, head_count, HEAD), 2, 0), jnp.moveaxis(dout_tiles.reshape(tile_count, tile_size, head_count, HEAD), 2, 0), jnp.moveaxis(window_key, 2, 0), jnp.moveaxis(window_value, 2, 0))
    query_out, attended, key_pool, value_pool = lax.map(per_head, heads_first)
    query_out = jnp.moveaxis(query_out, 0, 2).reshape(tile_count, tile_size, features)
    attended = jnp.moveaxis(attended, 0, 2).reshape(tile_count, tile_size, features)
    key_pool = jnp.moveaxis(key_pool, 0, 2).reshape(pool_count, tile_size, features)
    value_pool = jnp.moveaxis(value_pool, 0, 2).reshape(pool_count, tile_size, features)
    return (query_out, attended, key_pool, value_pool)

def reference(queries, key_states, value_states, out_grad, out_weight, win_time, win_space, tile_len):
    clip_count, token_count, features = queries.shape
    out_width = out_grad.shape[2]
    slab_count = N_TM
    tile_count = token_count // slab_count // TILE
    head_grad = jnp.dot(out_grad.reshape(-1, out_width), out_weight, preferred_element_type=jnp.float32).astype(jnp.bfloat16)
    tiled_shape = (clip_count, slab_count, tile_count, TILE, features)
    query_tiles = queries.reshape(tiled_shape)
    dout_tiles = head_grad.reshape(tiled_shape)
    key_tiles = key_states.reshape(tiled_shape)
    value_tiles = value_states.reshape(tiled_shape)
    len_tiles = tile_len.reshape(clip_count, slab_count, tile_count)
    time_tiles = win_time.reshape(clip_count, slab_count, tile_count, -1)
    space_tiles = win_space.reshape(clip_count, slab_count, tile_count, -1)
    centre = tile_count + lax.broadcasted_iota(jnp.int32, (tile_count, 1), 0)

    def item_grads(item_index):
        clip_index = item_index // slab_count
        slab_index = item_index % slab_count
        before = (slab_index + slab_count - 1) % slab_count
        later = (slab_index + 1) % slab_count
        pool_key = jnp.concatenate((key_tiles[clip_index, before], key_tiles[clip_index, slab_index], key_tiles[clip_index, later]), axis=0)
        pool_value = jnp.concatenate((value_tiles[clip_index, before], value_tiles[clip_index, slab_index], value_tiles[clip_index, later]), axis=0)
        pool_len = jnp.concatenate((len_tiles[clip_index, before], len_tiles[clip_index, slab_index], len_tiles[clip_index, later]), axis=0)
        further = (time_tiles[clip_index, slab_index] + 1) * tile_count + space_tiles[clip_index, slab_index]
        slot_codes = jnp.concatenate((centre, further), axis=1).astype(jnp.int32)
        query_out, attended, key_pool, value_pool = slab_grads(query_tiles[clip_index, slab_index], dout_tiles[clip_index, slab_index], pool_key, pool_value, pool_len, slot_codes)
        return (query_out, attended, key_pool[tile_count:2 * tile_count], value_pool[tile_count:2 * tile_count], key_pool[:tile_count].astype(jnp.bfloat16), value_pool[:tile_count].astype(jnp.bfloat16), key_pool[2 * tile_count:].astype(jnp.bfloat16), value_pool[2 * tile_count:].astype(jnp.bfloat16))
    items = jnp.arange(clip_count * slab_count, dtype=jnp.int32)
    results = lax.map(item_grads, items)
    shaped = [piece_all.reshape(tiled_shape) for piece_all in results]
    query_out, attended, key_own, value_own, key_prev, value_prev, key_next, value_next = shaped
    key_grad = key_own + jnp.roll(key_prev, -1, axis=1).astype(jnp.float32) + jnp.roll(key_next, 1, axis=1).astype(jnp.float32)
    value_grad = value_own + jnp.roll(value_prev, -1, axis=1).astype(jnp.float32) + jnp.roll(value_next, 1, axis=1).astype(jnp.float32)
    weight_grad = jnp.dot(out_grad.reshape(-1, out_width).T, attended.reshape(-1, features), preferred_element_type=jnp.float32)
    full_shape = (clip_count, token_count, features)
    return (query_out.reshape(full_shape), key_grad.astype(jnp.bfloat16).reshape(full_shape), value_grad.astype(jnp.bfloat16).reshape(full_shape), weight_grad)
```

```python
import functools
import math

import jax
import jax.numpy as jnp
from jax import lax
from jax.experimental import pallas as pl
from jax.experimental.pallas import tpu as pltpu
from jax.sharding import PartitionSpec as P

HEAD = 128
TILE = 384
SLOTS = 4
GROUPS = 4

NT = (((1,), (1,)), ((), ()))
NN = (((1,), (0,)), ((), ()))


def mm(a, b, dims=NN):
    return lax.dot_general(a, b, dims, preferred_element_type=jnp.float32)


def passed_along(array, axis, by):
    size = lax.axis_size(axis)
    return lax.ppermute(array, axis, [(i, (i + by) % size) for i in range(size)])


def attention_kernel(
    codes_ref, lens_ref, q_ref, do_ref, kp_ref, k_ref, kn_ref, vp_ref, v_ref, vn_ref,
    dq_ref, att_ref, to_prev_ref, own_ref, to_next_ref,
    kpool, vpool, ktp, vtp, dkp, dvp, p_ref, pb_ref, *, tiles
):
    pool = 3 * tiles
    scale = 1.0 / math.sqrt(HEAD)
    to_base2 = scale * math.log2(math.e)
    for side, (kr, vr) in enumerate(((kp_ref, vp_ref), (k_ref, v_ref), (kn_ref, vn_ref))):
        for j in range(tiles):
            at = side * tiles + j
            kt = kr[0, j * TILE:(j + 1) * TILE, :]
            vt = vr[0, j * TILE:(j + 1) * TILE, :]
            kpool[at] = kt
            vpool[at] = vt
            ktp[at] = kt.T
            vtp[at] = vt.T
    dkp[...] = jnp.zeros_like(dkp)
    dvp[...] = jnp.zeros_like(dvp)
    half = TILE // 2
    for t in range(tiles):
        rows = slice(t * TILE, (t + 1) * TILE)
        q = q_ref[0, rows, :]
        do = do_ref[rows, :]
        doT = do.T
        codes = [codes_ref[t * SLOTS + w] for w in range(SLOTS)]
        top = None
        for w in range(SLOTS):
            s = mm(kpool[codes[w]], q, NT)
            lower = s[half:]
            key = half + lax.broadcasted_iota(jnp.int32, lower.shape, 0)
            lower = jnp.where(key < lens_ref[t * SLOTS + w], lower, -jnp.inf)
            p_ref[t, w, :half, :] = s[:half]
            p_ref[t, w, half:, :] = lower
            here = jnp.max(jnp.maximum(s[:half], lower), axis=0, keepdims=True)
            top = here if top is None else jnp.maximum(top, here)
        total = jnp.zeros_like(top)
        for w in range(SLOTS):
            e = jnp.exp2((p_ref[t, w] - top) * to_base2)
            p_ref[t, w] = e
            total = total + jnp.sum(e, axis=0, keepdims=True)
        inv = 1.0 / total
        oT = jnp.zeros((HEAD, TILE), jnp.float32)
        for w in range(SLOTS):
            p = p_ref[t, w] * inv
            p_ref[t, w] = p
            pb = p.astype(jnp.bfloat16)
            pb_ref[t, w] = pb
            oT = oT + mm(vtp[codes[w]], pb)
        attT = oT.astype(jnp.bfloat16).astype(jnp.float32)
        att_ref[rows, :] = attT.T.astype(jnp.bfloat16)
        rowdot = jnp.sum(doT.astype(jnp.float32) * attT, axis=0, keepdims=True)
        dqT = jnp.zeros((HEAD, TILE), jnp.float32)
        for w in range(SLOTS):
            dp = mm(vpool[codes[w]], do, NT)
            ds = (p_ref[t, w] * (dp - rowdot)).astype(jnp.bfloat16)
            dqT = dqT + mm(ktp[codes[w]], ds)
            dkp[codes[w]] += mm(ds, q)
            dvp[codes[w]] += mm(pb_ref[t, w], do)
        dq_ref[rows, :] = (dqT * scale).T.astype(jnp.bfloat16)
    for j in range(tiles):
        rows = slice(j * TILE, (j + 1) * TILE)
        to_prev_ref[0, rows, :] = (dkp[j] * scale).astype(jnp.bfloat16)
        to_prev_ref[1, rows, :] = dvp[j].astype(jnp.bfloat16)
        own_ref[0, rows, :] = dkp[tiles + j] * scale
        own_ref[1, rows, :] = dvp[tiles + j]
        to_next_ref[0, rows, :] = (dkp[2 * tiles + j] * scale).astype(jnp.bfloat16)
        to_next_ref[1, rows, :] = dvp[2 * tiles + j].astype(jnp.bfloat16)


def attention(first, heads, codes, lens, queries, head_grad, prev, key_states, value_states, nxt):
    tokens = queries.shape[1]
    tiles = tokens // TILE
    pool = 3 * tiles
    width = heads * HEAD
    whole = pl.BlockSpec((1, tokens, HEAD), lambda h, *_: (0, 0, first + h))
    key_half = pl.BlockSpec((1, tokens, HEAD), lambda h, *_: (0, 0, h))
    value_half = pl.BlockSpec((1, tokens, HEAD), lambda h, *_: (1, 0, h))
    rows_whole = pl.BlockSpec((tokens, HEAD), lambda h, *_: (0, first + h))
    rows_part = pl.BlockSpec((tokens, HEAD), lambda h, *_: (0, h))
    pair = pl.BlockSpec((2, tokens, HEAD), lambda h, *_: (0, 0, h))
    pairs = tiles * SLOTS * TILE * TILE * HEAD * heads
    return pl.pallas_call(
        functools.partial(attention_kernel, tiles=tiles),
        grid_spec=pltpu.PrefetchScalarGridSpec(
            num_scalar_prefetch=2,
            grid=(heads,),
            in_specs=[whole, rows_whole, key_half, whole, key_half, value_half, whole, value_half],
            out_specs=[rows_part, rows_part, pair, pair, pair],
            scratch_shapes=[
                pltpu.VMEM((pool, TILE, HEAD), jnp.bfloat16),
                pltpu.VMEM((pool, TILE, HEAD), jnp.bfloat16),
                pltpu.VMEM((pool, HEAD, TILE), jnp.bfloat16),
                pltpu.VMEM((pool, HEAD, TILE), jnp.bfloat16),
                pltpu.VMEM((pool, TILE, HEAD), jnp.float32),
                pltpu.VMEM((pool, TILE, HEAD), jnp.float32),
                pltpu.VMEM((tiles, SLOTS, TILE, TILE), jnp.float32),
                pltpu.VMEM((tiles, SLOTS, TILE, TILE), jnp.bfloat16),
            ],
        ),
        out_shape=[
            jax.ShapeDtypeStruct((tokens, width), jnp.bfloat16),
            jax.ShapeDtypeStruct((tokens, width), jnp.bfloat16),
            jax.ShapeDtypeStruct((2, tokens, width), jnp.bfloat16),
            jax.ShapeDtypeStruct((2, tokens, width), jnp.float32),
            jax.ShapeDtypeStruct((2, tokens, width), jnp.bfloat16),
        ],
        compiler_params=pltpu.CompilerParams(
            dimension_semantics=("arbitrary",), vmem_limit_bytes=48 * 1024 * 1024
        ),
        cost_estimate=pl.CostEstimate(
            flops=24 * pairs, bytes_accessed=12 * tokens * width * 2, transcendentals=0
        ),
    )(codes, lens, queries, head_grad, prev, key_states, nxt, prev, value_states, nxt)


def scattered_sum(parts):
    tm, dp = lax.axis_size("tm"), lax.axis_size("dp")
    here, depth = lax.axis_index("tm"), lax.axis_index("dp")
    rows, columns = parts.shape
    block = rows // (tm * dp)
    held = parts.reshape(tm // 2, 2, dp * block, columns)

    def halve(held, bit):
        mine = (here >> bit) % 2
        away = lax.dynamic_index_in_dim(held, 1 - mine, 1, keepdims=False)
        kept = lax.dynamic_index_in_dim(held, mine, 1, keepdims=False)
        step = 1 << bit
        came = lax.ppermute(away.astype(jnp.bfloat16), "tm", [(i, i ^ step) for i in range(tm)])
        return kept.astype(jnp.float32) + came.astype(jnp.float32)

    held = halve(held, 0)
    held = held.reshape(tm // 2, dp, block, columns)
    total = lax.dynamic_index_in_dim(held, depth, 1, keepdims=False)
    for by in range(1, dp):
        target = (depth + by) % dp
        away = lax.dynamic_index_in_dim(held, target, 1, keepdims=False).astype(jnp.bfloat16)
        total = total + passed_along(away, "dp", by).astype(jnp.float32)
    held = total
    bit, groups = 1, tm // 2
    while groups > 1:
        held = halve(held.reshape(groups // 2, 2, block, columns), bit)
        groups //= 2
        bit += 1
    return held.reshape(block, columns)


def shards(queries, key_states, value_states, out_grad, out_weight, win_time, win_space, tile_len):
    tokens = queries.shape[1]
    features = queries.shape[2]
    tiles = tokens // TILE
    head_count = features // HEAD
    heads = head_count // GROUPS
    width = heads * HEAD
    slab_count = lax.axis_size("tm")
    slab_index = lax.axis_index("tm")
    all_len = tile_len[0]
    pool_len = jnp.concatenate(
        [
            lax.dynamic_slice_in_dim(
                all_len, (slab_index + offset + slab_count) % slab_count * tiles, tiles
            )
            for offset in (-1, 0, 1)
        ]
    )
    centre = tiles + lax.broadcasted_iota(jnp.int32, (tiles, 1), 0)
    codes = jnp.concatenate((centre, (win_time[0] + 1) * tiles + win_space[0]), axis=1).reshape(-1)
    lens = jnp.sum(
        jnp.where(
            codes[:, None] == lax.broadcasted_iota(jnp.int32, (codes.shape[0], 3 * tiles), 1),
            pool_len[None, :],
            0,
        ),
        axis=1,
    )
    rows_in = out_grad[0]
    arrived = []
    for g in range(GROUPS):
        part = slice(g * width, (g + 1) * width)
        both = jnp.stack((key_states[0, :, part], value_states[0, :, part]))
        arrived.append((passed_along(both, "tm", 1), passed_along(both, "tm", -1)))
    head_grad = jnp.dot(
        rows_in,
        lax.all_gather(out_weight, "dp", axis=0, tiled=True),
        preferred_element_type=jnp.float32,
    ).astype(jnp.bfloat16)
    query_parts, attended_parts, grads = [], [], []
    for g in range(GROUPS):
        prev, nxt = arrived[g]
        dq, att, to_prev, own, to_next = attention(
            g * heads, heads, codes, lens, queries, head_grad, prev, key_states, value_states, nxt
        )
        from_next = passed_along(to_prev, "tm", -1)
        from_prev = passed_along(to_next, "tm", 1)
        query_parts.append(dq)
        attended_parts.append(att)
        grads.append((own, from_next, from_prev))
    attended = jnp.concatenate(attended_parts, axis=1)
    weight_grad = scattered_sum(
        lax.dot_general(
            rows_in, attended, (((0,), (0,)), ((), ())), preferred_element_type=jnp.float32
        )
    )
    summed = [
        (own + a.astype(jnp.float32) + b.astype(jnp.float32)).astype(jnp.bfloat16)
        for own, a, b in grads
    ]
    full_shape = (1, tokens, features)
    return (
        jnp.concatenate(query_parts, axis=1).reshape(full_shape),
        jnp.concatenate([s[0] for s in summed], axis=1).reshape(full_shape),
        jnp.concatenate([s[1] for s in summed], axis=1).reshape(full_shape),
        weight_grad,
    )


def solution(mesh):
    in_specs = (
        P("dp", "tm", None),
        P("dp", "tm", None),
        P("dp", "tm", None),
        P("dp", "tm", None),
        P("dp", None),
        P("dp", "tm", None),
        P("dp", "tm", None),
        P("dp", None),
    )
    out_specs = (
        P("dp", "tm", None),
        P("dp", "tm", None),
        P("dp", "tm", None),
        P(("tm", "dp"), None),
    )
    return jax.shard_map(shards, mesh=mesh, in_specs=in_specs, out_specs=out_specs, check_vma=False)
```

```python
import functools
import math

import jax
import jax.numpy as jnp
from jax import lax
from jax.experimental import pallas as pl
from jax.experimental.pallas import tpu as pltpu
from jax.sharding import PartitionSpec as P

HEAD = 128
TILE = 384
SLOTS = 4
GROUPS = 4
BATCHES = ((0, 1), (1, 2), (2, 4))

NT = (((1,), (1,)), ((), ()))
NN = (((1,), (0,)), ((), ()))


def mm(a, b, dims=NN):
    return lax.dot_general(a, b, dims, preferred_element_type=jnp.float32)


def passed_along(array, axis, by):
    size = lax.axis_size(axis)
    return lax.ppermute(array, axis, [(i, (i + by) % size) for i in range(size)])


def attention_kernel(
    codes_ref, lens_ref, q_ref, do_ref, kp_ref, k_ref, kn_ref, vp_ref, v_ref, vn_ref,
    dq_ref, att_ref, to_prev_ref, own_ref, to_next_ref,
    kpool, vpool, ktp, vtp, dkp, dvp, p_ref, pb_ref, *, tiles
):
    pool = 3 * tiles
    scale = 1.0 / math.sqrt(HEAD)
    to_base2 = scale * math.log2(math.e)
    for side, (kr, vr) in enumerate(((kp_ref, vp_ref), (k_ref, v_ref), (kn_ref, vn_ref))):
        for j in range(tiles):
            at = side * tiles + j
            kt = kr[0, j * TILE:(j + 1) * TILE, :]
            vt = vr[0, j * TILE:(j + 1) * TILE, :]
            kpool[at] = kt
            vpool[at] = vt
            ktp[at] = kt.T
            vtp[at] = vt.T
    dkp[...] = jnp.zeros_like(dkp)
    dvp[...] = jnp.zeros_like(dvp)
    half = TILE // 2
    for t in range(tiles):
        rows = slice(t * TILE, (t + 1) * TILE)
        q = q_ref[0, rows, :]
        do = do_ref[rows, :]
        doT = do.T
        codes = [codes_ref[t * SLOTS + w] for w in range(SLOTS)]
        top = None
        for w in range(SLOTS):
            s = mm(kpool[codes[w]], q, NT)
            lower = s[half:]
            key = half + lax.broadcasted_iota(jnp.int32, lower.shape, 0)
            lower = jnp.where(key < lens_ref[t * SLOTS + w], lower, -jnp.inf)
            p_ref[t, w, :half, :] = s[:half]
            p_ref[t, w, half:, :] = lower
            here = jnp.max(jnp.maximum(s[:half], lower), axis=0, keepdims=True)
            top = here if top is None else jnp.maximum(top, here)
        total = jnp.zeros_like(top)
        for w in range(SLOTS):
            e = jnp.exp2((p_ref[t, w] - top) * to_base2)
            p_ref[t, w] = e
            total = total + jnp.sum(e, axis=0, keepdims=True)
        inv = 1.0 / total
        oT = jnp.zeros((HEAD, TILE), jnp.float32)
        for w in range(SLOTS):
            p = p_ref[t, w] * inv
            p_ref[t, w] = p
            pb = p.astype(jnp.bfloat16)
            pb_ref[t, w] = pb
            oT = oT + mm(vtp[codes[w]], pb)
        attT = oT.astype(jnp.bfloat16).astype(jnp.float32)
        att_ref[rows, :] = attT.T.astype(jnp.bfloat16)
        rowdot = jnp.sum(doT.astype(jnp.float32) * attT, axis=0, keepdims=True)
        dqT = jnp.zeros((HEAD, TILE), jnp.float32)
        for w in range(SLOTS):
            dp = mm(vpool[codes[w]], do, NT)
            ds = (p_ref[t, w] * (dp - rowdot)).astype(jnp.bfloat16)
            dqT = dqT + mm(ktp[codes[w]], ds)
            dkp[codes[w]] += mm(ds, q)
            dvp[codes[w]] += mm(pb_ref[t, w], do)
        dq_ref[rows, :] = (dqT * scale).T.astype(jnp.bfloat16)
    for j in range(tiles):
        rows = slice(j * TILE, (j + 1) * TILE)
        to_prev_ref[0, rows, :] = (dkp[j] * scale).astype(jnp.bfloat16)
        to_prev_ref[1, rows, :] = dvp[j].astype(jnp.bfloat16)
        own_ref[0, rows, :] = dkp[tiles + j] * scale
        own_ref[1, rows, :] = dvp[tiles + j]
        to_next_ref[0, rows, :] = (dkp[2 * tiles + j] * scale).astype(jnp.bfloat16)
        to_next_ref[1, rows, :] = dvp[2 * tiles + j].astype(jnp.bfloat16)


def attention(first, offset, heads, codes, lens, queries, head_grad, prev, key_states, value_states, nxt):
    tokens = queries.shape[1]
    tiles = tokens // TILE
    pool = 3 * tiles
    width = heads * HEAD
    whole = pl.BlockSpec((1, tokens, HEAD), lambda h, *_: (0, 0, first + h))
    key_half = pl.BlockSpec((1, tokens, HEAD), lambda h, *_: (0, 0, offset + h))
    value_half = pl.BlockSpec((1, tokens, HEAD), lambda h, *_: (1, 0, offset + h))
    rows_whole = pl.BlockSpec((tokens, HEAD), lambda h, *_: (0, first + h))
    rows_part = pl.BlockSpec((tokens, HEAD), lambda h, *_: (0, h))
    pair = pl.BlockSpec((2, tokens, HEAD), lambda h, *_: (0, 0, h))
    pairs = tiles * SLOTS * TILE * TILE * HEAD * heads
    return pl.pallas_call(
        functools.partial(attention_kernel, tiles=tiles),
        grid_spec=pltpu.PrefetchScalarGridSpec(
            num_scalar_prefetch=2,
            grid=(heads,),
            in_specs=[whole, rows_whole, key_half, whole, key_half, value_half, whole, value_half],
            out_specs=[rows_part, rows_part, pair, pair, pair],
            scratch_shapes=[
                pltpu.VMEM((pool, TILE, HEAD), jnp.bfloat16),
                pltpu.VMEM((pool, TILE, HEAD), jnp.bfloat16),
                pltpu.VMEM((pool, HEAD, TILE), jnp.bfloat16),
                pltpu.VMEM((pool, HEAD, TILE), jnp.bfloat16),
                pltpu.VMEM((pool, TILE, HEAD), jnp.float32),
                pltpu.VMEM((pool, TILE, HEAD), jnp.float32),
                pltpu.VMEM((tiles, SLOTS, TILE, TILE), jnp.float32),
                pltpu.VMEM((tiles, SLOTS, TILE, TILE), jnp.bfloat16),
            ],
        ),
        out_shape=[
            jax.ShapeDtypeStruct((tokens, width), jnp.bfloat16),
            jax.ShapeDtypeStruct((tokens, width), jnp.bfloat16),
            jax.ShapeDtypeStruct((2, tokens, width), jnp.bfloat16),
            jax.ShapeDtypeStruct((2, tokens, width), jnp.float32),
            jax.ShapeDtypeStruct((2, tokens, width), jnp.bfloat16),
        ],
        compiler_params=pltpu.CompilerParams(
            dimension_semantics=("arbitrary",), vmem_limit_bytes=48 * 1024 * 1024
        ),
        cost_estimate=pl.CostEstimate(
            flops=2 * pairs, bytes_accessed=tokens * width, transcendentals=0
        ),
    )(codes, lens, queries, head_grad, prev, key_states, nxt, prev, value_states, nxt)


def across(array, axis, bit):
    size = lax.axis_size(axis)
    return lax.ppermute(array, axis, [(i, i ^ (1 << bit)) for i in range(size)])


def halved(held, bit):
    mine = (lax.axis_index("tm") >> bit) % 2
    away = lax.dynamic_index_in_dim(held, 1 - mine, 1, keepdims=False)
    kept = lax.dynamic_index_in_dim(held, mine, 1, keepdims=False)
    came = across(away.astype(jnp.bfloat16), "tm", bit)
    return kept.astype(jnp.float32) + came.astype(jnp.float32)


def summed_over_cores(parts):
    tm, dp = lax.axis_size("tm"), lax.axis_size("dp")
    rows, columns = parts.shape
    held = halved(parts.reshape(tm // 2, 2, rows // tm, columns), 0)
    return held.reshape(tm // 2, dp, rows // (tm * dp), columns)


def summed_over_dp(held):
    dp, depth = lax.axis_size("dp"), lax.axis_index("dp")
    total = lax.dynamic_index_in_dim(held, depth, 1, keepdims=False)
    for by in range(1, dp):
        away = lax.dynamic_index_in_dim(held, (depth + by) % dp, 1, keepdims=False)
        total = total + passed_along(away.astype(jnp.bfloat16), "dp", by).astype(jnp.float32)
    return total


def summed_over_rest(held):
    groups, block, columns = held.shape
    bit = 1
    while groups > 1:
        groups //= 2
        held = halved(held.reshape(groups, 2, block, columns), bit)
        bit += 1
    return held.reshape(block, columns)


def whole_weight(out_weight, first_keys):
    rows, columns = out_weight.shape
    core = lax.axis_index("tm") % 2
    halves = out_weight.reshape(2, rows // 2, columns)
    mine = lax.all_gather(
        lax.dynamic_index_in_dim(halves, core, 0, keepdims=False), "dp", axis=0, tiled=False
    )
    mine, first_keys = lax.optimization_barrier((mine, first_keys))
    other = across(mine, "tm", 0)
    first = jnp.where(core == 0, mine, other)
    second = jnp.where(core == 0, other, mine)
    return jnp.stack((first, second), axis=1).reshape(-1, columns), first_keys


def shards(queries, key_states, value_states, out_grad, out_weight, win_time, win_space, tile_len):
    tokens = queries.shape[1]
    features = queries.shape[2]
    tiles = tokens // TILE
    head_count = features // HEAD
    heads = head_count // GROUPS
    width = heads * HEAD
    slab_count = lax.axis_size("tm")
    slab_index = lax.axis_index("tm")
    all_len = tile_len[0]
    pool_len = jnp.concatenate(
        [
            lax.dynamic_slice_in_dim(
                all_len, (slab_index + offset + slab_count) % slab_count * tiles, tiles
            )
            for offset in (-1, 0, 1)
        ]
    )
    centre = tiles + lax.broadcasted_iota(jnp.int32, (tiles, 1), 0)
    codes = jnp.concatenate((centre, (win_time[0] + 1) * tiles + win_space[0]), axis=1).reshape(-1)
    lens = jnp.sum(
        jnp.where(
            codes[:, None] == lax.broadcasted_iota(jnp.int32, (codes.shape[0], 3 * tiles), 1),
            pool_len[None, :],
            0,
        ),
        axis=1,
    )
    rows_in = out_grad[0]
    arrived = []
    for begin, end in BATCHES:
        part = slice(begin * width, end * width)
        both = jnp.stack((key_states[0, :, part], value_states[0, :, part]))
        arrived.append((passed_along(both, "tm", 1), passed_along(both, "tm", -1)))
    weight, arrived[0] = whole_weight(out_weight, arrived[0])
    head_grad = jnp.dot(rows_in, weight, preferred_element_type=jnp.float32).astype(jnp.bfloat16)
    query_parts, attended_parts, grads = [], [], []
    held = total = None

    def weight_terms(parts):
        return lax.dot_general(
            rows_in,
            jnp.concatenate(parts, axis=1),
            (((0,), (0,)), ((), ())),
            preferred_element_type=jnp.float32,
        )

    for g in range(GROUPS):
        batch = [begin <= g < end for begin, end in BATCHES].index(True)
        prev, nxt = arrived[batch]
        offset = (g - BATCHES[batch][0]) * heads
        if g == GROUPS - 1:
            held, nxt, grads[0] = lax.optimization_barrier((held, nxt, grads[0]))
            total = summed_over_dp(held)
        dq, att, to_prev, own, to_next = attention(
            g * heads, offset, heads, codes, lens,
            queries, head_grad, prev, key_states, value_states, nxt,
        )
        from_next = passed_along(to_prev, "tm", -1)
        from_prev = passed_along(to_next, "tm", 1)
        query_parts.append(dq)
        attended_parts.append(att)
        grads.append((own, from_next, from_prev))
        if g == GROUPS // 2 - 1:
            held = summed_over_cores(weight_terms(attended_parts))
    last_parts, total = lax.optimization_barrier((attended_parts[GROUPS // 2:], total))
    total_last = summed_over_dp(summed_over_cores(weight_terms(last_parts)))
    weight_grad = summed_over_rest(jnp.concatenate((total, total_last), axis=2))
    summed = [
        (own + a.astype(jnp.float32) + b.astype(jnp.float32)).astype(jnp.bfloat16)
        for own, a, b in grads
    ]
    full_shape = (1, tokens, features)
    return (
        jnp.concatenate(query_parts, axis=1).reshape(full_shape),
        jnp.concatenate([s[0] for s in summed], axis=1).reshape(full_shape),
        jnp.concatenate([s[1] for s in summed], axis=1).reshape(full_shape),
        weight_grad,
    )


def solution(mesh):
    in_specs = (
        P("dp", "tm", None),
        P("dp", "tm", None),
        P("dp", "tm", None),
        P("dp", "tm", None),
        P("dp", None),
        P("dp", "tm", None),
        P("dp", "tm", None),
        P("dp", None),
    )
    out_specs = (
        P("dp", "tm", None),
        P("dp", "tm", None),
        P("dp", "tm", None),
        P(("tm", "dp"), None),
    )
    return jax.shard_map(shards, mesh=mesh, in_specs=in_specs, out_specs=out_specs, check_vma=False)
```
